32 devices in a mesh: groups: 2 (over y), atoms: 16 (over z, x, core).
Axes of the slice: x: 2, y: 2, z: 4, core: 2. Of those that a mesh axis runs over, the one named last changes fastest.
Arguments:
- particle_coordinates: float32 [3, 4096], P(None, ('groups', 'atoms')), parts along dimension 1, may hold values from 0 to 72
- integer_lattice_modes: int32 [3, 4096], replicated, may hold values from -6 to 6
- hidden_embeddings: bfloat16 [2, 4096, 128], P(None, ('groups', 'atoms')), parts along dimension 1, may hold values from -6 to 6
- cached_density_modes: bfloat16 [4, 4096, 256], P('groups'), parts along dimension 0, may hold values from -6 to 6
- spectral_kernels: bfloat16 [2, 4096, 128], replicated, may hold values from -4 to 4
- final_embedding_adjoint: bfloat16 [4096, 128], P(('groups', 'atoms')), parts along dimension 0, may hold values from -6 to 6
- particle_result_line: int32 [4096], P(('groups', 'atoms')), parts along dimension 0, may hold values from 0 to 2047, as said below
Outputs:
- feat_grad: float32 [4096, 128], P(('groups', 'atoms')), parts along dimension 0
- pos_grad: float32 [3, 4096], P(None, ('groups', 'atoms')), parts along dimension 1
- filter_grad: float32 [2, 8192, 128], P(None, ('groups', 'atoms')), parts along dimension 1
The draws below stay inside these ranges and needn't reach their ends.
There are 2 independent parts, one for each index of `groups`. The reference program is written for one: setup_inputs(seed, part) draws one part's arguments, and reference() takes and returns one part's arrays. A program takes and returns all parts, laid end to end along the dimension named above; an argument that names none is the same for every part. Nothing has to cross between parts.
Inputs may be any that keep to these rules, and one draw needn't show every extreme that they name: `particle_result_line`: a permutation of the atoms; the atoms of each aligned block of 128 rows send exactly the same number of atoms to every aligned block of 128 output rows.
All inputs are finite; a program needn't handle non-finite values.
Results may differ from the reference program's by a relative error of at most 0.0075.
Values may be sent and summed in bfloat16 or wider, within the bound.
A program may use at most 128 MiB of HBM per device.

```python
import math
import jax
import jax.numpy as jnp
from jax import lax

CH = 128
LATTICE_WAVES = 4096
BLOCKS = 2
BOX = 72
A_DEV = 128
ATOMS = 2048


def permute_one(key_item, base_list):
    return jax.random.permutation(key_item, base_list)


def draw_particle_result_line(key, part):
    blocks = ATOMS // A_DEV
    per_block = A_DEV // blocks
    base_list = jnp.repeat(jnp.arange(blocks, dtype=jnp.int32), per_block)
    key_list = jax.random.split(jax.random.fold_in(key, 11), blocks)
    target = jax.vmap(permute_one, in_axes=(0, None))(key_list, base_list).reshape(-1)
    onehot = (target[:, None] == jnp.arange(blocks, dtype=jnp.int32)[None, :]).astype(jnp.int32)
    ranking = jnp.sum(jnp.cumsum(onehot, axis=0) * onehot, axis=1) - 1
    slot_keys = jax.random.split(jax.random.fold_in(key, 23), blocks)
    tables = jax.vmap(permute_one, in_axes=(0, None))(slot_keys, jnp.arange(A_DEV, dtype=jnp.int32))
    slot_pos = tables[target, ranking]
    return (target * A_DEV + slot_pos).astype(jnp.int32)


def plant(entries, rng, smallest, largest):
    spot = [jax.random.randint(jax.random.fold_in(rng, axis), (), 0, length) for axis, length in enumerate(entries.shape)]
    widest = entries.shape.index(max(entries.shape))
    next_to = spot[:widest] + [(spot[widest] + 1) % entries.shape[widest]] + spot[widest + 1:]
    return entries.at[tuple(spot)].set(smallest).at[tuple(next_to)].set(largest)


def level_of(rng, shape, cuts, least, high):
    factor_of = 1.0
    for axis_at, blocks in cuts:
        draws = jax.random.uniform(jax.random.fold_in(jax.random.fold_in(rng, 6), axis_at), (blocks,), jnp.float32, least / len(cuts), high / len(cuts))
        factor_of = factor_of * jnp.repeat(jnp.exp(draws), shape[axis_at] // blocks).reshape((-1,) + (1,) * (len(shape) - 1 - axis_at))
    return factor_of


def bell_draw(rng, dims, deviation, most, shards=(), kind=jnp.bfloat16):
    loudness = level_of(rng, dims, shards, -0.22, 0.18) if shards else 1.0
    array = jax.random.normal(rng, dims, jnp.float32) * deviation * loudness
    return jnp.minimum(jnp.maximum(array, -most), most).astype(kind)


def setup_inputs(seed: int = 0, part: int = 0) -> dict:
    arg_keys = jax.random.split(jax.random.key(seed), 8)
    own_keys = jax.random.split(jax.random.fold_in(arg_keys[7], part), 8)
    return {
        "particle_coordinates": jnp.clip(72.0 * jax.random.uniform(own_keys[0], (3, ATOMS), jnp.float32) ** level_of(own_keys[0], (3, ATOMS), ((1, 16),), -0.2, 0.2), 0.0, 72.0),
        "integer_lattice_modes": plant(jax.random.randint(arg_keys[1], (3, LATTICE_WAVES), -6, 7), jax.random.fold_in(arg_keys[1], 1), -6, 6).astype(jnp.int32),
        "hidden_embeddings": bell_draw(own_keys[2], (BLOCKS, ATOMS, CH), 1.0, 6.0, ((1, 16),)),
        "cached_density_modes": bell_draw(own_keys[3], (BLOCKS, LATTICE_WAVES, 2 * CH), 1.0, 6.0),
        "spectral_kernels": bell_draw(arg_keys[4], (BLOCKS, LATTICE_WAVES, CH), 1.0, 4.0),
        "final_embedding_adjoint": bell_draw(own_keys[5], (ATOMS, CH), 1.0, 6.0, ((0, 16),)),
        "particle_result_line": draw_particle_result_line(jax.random.fold_in(jax.random.fold_in(arg_keys[7], part), 71), part),
    }


def angle_terms(particle_locations, integer_lattice_modes):
    lattice_mode = integer_lattice_modes.astype(jnp.float32)
    angles = (particle_locations[0][:, None] * lattice_mode[0][None, :] + particle_locations[1][:, None] * lattice_mode[1][None, :] + particle_locations[2][:, None] * lattice_mode[2][None, :]) * (2.0 * math.pi / BOX)
    return jnp.cos(angles).astype(jnp.bfloat16), jnp.sin(angles).astype(jnp.bfloat16)


def silu_slope(values_in):
    logistic = jax.nn.sigmoid(values_in)
    return logistic * (1.0 + values_in * (1.0 - logistic))


def reference(particle_coordinates, integer_lattice_modes, hidden_embeddings, cached_density_modes, spectral_kernels, final_embedding_adjoint, particle_result_line):
    row_block = min(1024, ATOMS)
    row_count = ATOMS // row_block
    k_scale = LATTICE_WAVES ** -0.5
    a_scale = ATOMS ** -0.5
    two_pi_box = 2.0 * math.pi / BOX
    lattice_mode = integer_lattice_modes.astype(jnp.float32)
    coord_blocks = particle_coordinates.reshape(3, row_count, row_block).transpose(1, 0, 2)
    cotangent = final_embedding_adjoint.astype(jnp.float32)
    pos_total = jnp.zeros((3, ATOMS), jnp.float32)
    filter_parts = []
    for layer_index in range(BLOCKS - 1, -1, -1):
        feature = hidden_embeddings[layer_index]
        saved_block = cached_density_modes[layer_index].astype(jnp.float32)
        doubled = jnp.concatenate([spectral_kernels[layer_index], spectral_kernels[layer_index]], axis=1).astype(jnp.float32)
        filtered = (saved_block * doubled).astype(jnp.bfloat16)
        cot_blocks = cotangent.reshape(row_count, row_block, CH)

        def first_pass(adjoint, inputs):
            particle_locations, cot_rows = inputs
            even_trig_term, odd_trig_term = angle_terms(particle_locations, integer_lattice_modes)
            message = k_scale * (jnp.dot(even_trig_term, filtered[:, :CH], preferred_element_type=jnp.float32) + jnp.dot(odd_trig_term, filtered[:, CH:], preferred_element_type=jnp.float32))
            msg_grad = (cot_rows * silu_slope(message)).astype(jnp.bfloat16)
            adjoint = adjoint + jnp.concatenate([jnp.dot(even_trig_term.T, msg_grad, preferred_element_type=jnp.float32), jnp.dot(odd_trig_term.T, msg_grad, preferred_element_type=jnp.float32)], axis=1)
            return adjoint, msg_grad

        adjoint, msg_blocks = lax.scan(first_pass, jnp.zeros((LATTICE_WAVES, 2 * CH), jnp.float32), (coord_blocks, cot_blocks))
        adjoint = k_scale * adjoint
        filter_parts.append(adjoint[:, :CH] * saved_block[:, :CH] + adjoint[:, CH:] * saved_block[:, CH:])
        factor_grad = (adjoint * doubled).astype(jnp.bfloat16)
        feat_blocks = feature.reshape(row_count, row_block, CH)

        def second_pass(inputs):
            particle_locations, msg_grad, feat_rows = inputs
            even_trig_term, odd_trig_term = angle_terms(particle_locations, integer_lattice_modes)
            feat_add = a_scale * (jnp.dot(even_trig_term, factor_grad[:, :CH], preferred_element_type=jnp.float32) + jnp.dot(odd_trig_term, factor_grad[:, CH:], preferred_element_type=jnp.float32))
            cos_weight = k_scale * jnp.dot(msg_grad, filtered[:, :CH].T, preferred_element_type=jnp.float32) + a_scale * jnp.dot(feat_rows, factor_grad[:, :CH].T, preferred_element_type=jnp.float32)
            sin_weight = k_scale * jnp.dot(msg_grad, filtered[:, CH:].T, preferred_element_type=jnp.float32) + a_scale * jnp.dot(feat_rows, factor_grad[:, CH:].T, preferred_element_type=jnp.float32)
            dtheta = even_trig_term.astype(jnp.float32) * sin_weight - odd_trig_term.astype(jnp.float32) * cos_weight
            pos_add = two_pi_box * jnp.dot(lattice_mode, dtheta.T, precision=lax.Precision.HIGHEST)
            return feat_add, pos_add

        feat_add, pos_add = lax.map(second_pass, (coord_blocks, msg_blocks, feat_blocks))
        cotangent = cotangent + feat_add.reshape(ATOMS, CH)
        pos_total = pos_total + pos_add.transpose(1, 0, 2).reshape(3, ATOMS)
    filter_grad = jnp.stack(filter_parts[::-1])
    feat_grad = jnp.zeros((ATOMS, CH), jnp.float32).at[particle_result_line].set(cotangent)
    pos_grad = jnp.zeros((3, ATOMS), jnp.float32).at[:, particle_result_line].set(pos_total)
    return feat_grad, pos_grad, filter_grad
```

```python
import functools
import math

import jax
import jax.numpy as jnp
from jax import lax
from jax.experimental import pallas as pl
from jax.experimental.pallas import tpu as pltpu
from jax.sharding import PartitionSpec as P

BOX = 72
AXIS = "atoms"
F32, BF16 = jnp.float32, jnp.bfloat16
COS_TERMS = (0.999999212, -19.7389804, 64.9286585, -85.2716283, 58.7905066, -21.0711085)
SIN_TERMS = (6.28318492, -41.3415893, 81.5999439, -76.6144759, 41.3428894, -12.4712447)


def trig_of_turns(turns):
    part = turns - jnp.round(turns)
    square = part * part
    cos = COS_TERMS[-1]
    sin = SIN_TERMS[-1]
    for a in COS_TERMS[-2::-1]:
        cos = cos * square + a
    for a in SIN_TERMS[-2::-1]:
        sin = sin * square + a
    return cos.astype(BF16), (sin * part).astype(BF16)


def dot(a, b, ca=1, cb=0):
    return lax.dot_general(a, b, (((ca,), (cb,)), ((), ())), preferred_element_type=F32)


def repeat(count, step, most=8):
    if count <= most:
        for i in range(count):
            step(i)
    else:

        def run(i, carry):
            step(i)
            return carry

        lax.fori_loop(0, count, run, 0)


def pieces_of(rows):
    keep = lax.broadcasted_iota(jnp.int32, rows.shape, 0) < 3
    value = jnp.where(keep, rows * (1.0 / BOX), 0.0)
    high = value.astype(BF16).astype(F32)
    rest = value - high
    mid = rest.astype(BF16).astype(F32)
    return jnp.concatenate([high, mid, rest - mid, jnp.zeros_like(rows)], axis=0).astype(BF16)


def kernel(
    dims,
    coords_ref,
    modes_ref,
    hidden_ref,
    density_hbm,
    filter_hbm,
    cot_ref,
    line_ref,
    feat_ref,
    pos_ref,
    grad_ref,
    density,
    filters,
    meta,
    lattice,
    window,
    trig,
    wide,
    weights,
    fin,
    choose,
    message,
    slope,
    cot,
    partial,
    pos_sum,
    acc,
    s1,
    r1,
    s2,
    r2,
    s3,
    r3,
    load_sem,
    meta_send,
    meta_recv,
    hid_send,
    hid_recv,
    gat_send,
    gat_recv,
    s1_send,
    s1_recv,
    s2_send,
    s2_recv,
    s3_send,
    s3_recv,
):
    Z, X = dims
    n = Z * X * 2
    ch = cot_ref.shape[1]
    A = cot_ref.shape[0]
    modes = modes_ref.shape[1]
    own = modes // n
    atoms = n * A
    k_scale = modes ** (-0.5)
    a_scale = atoms ** (-0.5)
    me = lax.axis_index(AXIS)
    c = lax.rem(me, 2)
    x = lax.rem(me // 2, X)
    z = me // (2 * X)
    chunks = load_sem.shape[0]
    step_modes = modes // chunks

    def dev(zz, xx, cc):
        return (zz * X + xx) * 2 + cc

    def up(base, j, size):
        return lax.rem(base + j, size)

    def cols(d):
        return pl.ds(pl.multiple_of(d * A, A), A)

    def remote(src, dst, ssem, rsem, peer):
        return pltpu.make_async_remote_copy(
            src_ref=src,
            dst_ref=dst,
            send_sem=ssem,
            recv_sem=rsem,
            device_id={AXIS: peer},
            device_id_type=pl.DeviceIdType.MESH,
        )

    def loads(q):
        part = pl.ds(pl.multiple_of(q * step_modes, step_modes), step_modes)
        return (
            pltpu.make_async_copy(density_hbm.at[:, part], density.at[:, part], load_sem.at[q, 0]),
            pltpu.make_async_copy(filter_hbm.at[:, part], filters.at[:, part], load_sem.at[q, 1]),
        )

    def start_load(q):
        for copy in loads(q):
            copy.start()

    repeat(chunks, start_load)

    barrier = pltpu.get_barrier_semaphore()

    def greet(j):
        pl.semaphore_signal(
            barrier,
            inc=1,
            device_id={AXIS: up(me, j + 1, n)},
            device_id_type=pl.DeviceIdType.MESH,
        )

    repeat(n - 1, greet, 15)

    mine = cols(me)
    meta[:, mine] = jnp.zeros((8, A), F32)
    meta[0:3, mine] = coords_ref[...]
    meta[3:4, mine] = line_ref[...].astype(F32)
    for b in range(2):
        wide[b, ch : 2 * ch, mine] = hidden_ref[b].astype(F32).T.astype(BF16)
    pl.semaphore_wait(barrier, n - 1)

    def meta_copy(j):
        peer = up(me, j + 1, n)
        return remote(
            meta.at[:, mine], meta.at[:, mine], meta_send.at[j], meta_recv.at[j], peer
        )

    repeat(n - 1, lambda j: meta_copy(j).start(), 15)

    class Gather:
        def __init__(self, view, send, recv):
            self.view, self.send, self.recv = view, send, recv

        def copy(self, d, peer, k):
            return remote(self.view(d), self.view(d), self.send.at[k], self.recv.at[d], peer)

        def arrive(self, d):
            self.copy(d, up(me, 1, n), 0).wait_recv()

        def spread(self, d, j):
            for i in range(1, X):
                self.copy(d, dev(z, up(x, i, X), c), Z - 1 + j * (X - 1) + i - 1).start()
            self.copy(d, dev(z, x, 1 - c), Z - 1 + Z * (X - 1) + j * X).start()

        def start(self):
            repeat(
                Z - 1, lambda j: self.copy(me, dev(up(z, j + 1, Z), x, c), j).start()
            )
            self.spread(me, 0)

        def along_x(self):
            def step(j):
                d = dev(up(z, j + 1, Z), x, c)
                self.arrive(d)
                self.spread(d, j + 1)

            repeat(Z - 1, step)

        def along_core(self):
            def step(j):
                for i in range(1, X):
                    d = dev(up(z, j, Z), up(x, i, X), c)
                    self.arrive(d)
                    self.copy(d, dev(z, x, 1 - c), Z - 1 + Z * (X - 1) + j * X + i).start()

            repeat(Z, step)

        def finish(self):
            def step(j):
                for i in range(X):
                    self.arrive(dev(up(z, j, Z), up(x, i, X), 1 - c))

            repeat(Z, step)
            repeat(n - 1, lambda k: self.copy(me, up(me, 1, n), k).wait_send(), 15)

    hidden = Gather(lambda d: wide.at[:, pl.ds(ch, ch), cols(d)], hid_send, hid_recv)
    grads = [
        Gather(lambda d, b=b: wide.at[b, pl.ds(0, ch), cols(d)], gat_send, gat_recv)
        for b in range(2)
    ]
    final = Gather(lambda d: fin.at[:, cols(d)], gat_send, gat_recv)
    hidden.start()

    eight = jnp.concatenate(
        [modes_ref[...].astype(F32), jnp.zeros((5, modes), F32)], axis=0
    )
    lattice[...] = jnp.concatenate([eight, eight, eight, jnp.zeros_like(eight)], axis=0)
    my_pieces = pieces_of(meta[:, mine])
    message[...] = jnp.zeros_like(message)

    def message_step(q):
        part = pl.ds(pl.multiple_of(q * step_modes, step_modes), step_modes)
        cos, sin = trig_of_turns(dot(my_pieces, lattice[:, part].astype(BF16), 0, 0))
        for copy in loads(q):
            copy.wait()
        even, odd = [], []
        for b in range(2):
            factor = filters[b, part, :]
            even.append(density[b, part, 0:ch] * factor)
            odd.append(density[b, part, ch : 2 * ch] * factor)
        message[...] += dot(cos, jnp.concatenate(even, axis=1)) + dot(
            sin, jnp.concatenate(odd, axis=1)
        )

    repeat(chunks, message_step, 0)

    for b in range(2):
        value = k_scale * message[:, b * ch : (b + 1) * ch]
        logistic = 1.0 / (1.0 + jnp.exp(-value))
        slope[b] = (logistic * (1.0 + value * (1.0 - logistic))).T
    cot[...] = cot_ref[...].astype(F32).T
    wide[1, 0:ch, mine] = (cot[...] * slope[1]).astype(BF16)
    grads[1].start()
    hidden.along_x()

    repeat(n - 1, lambda j: meta_copy(j).wait_recv(), 15)
    width = window.shape[0]
    base = (me * own) // width * width
    near = lattice[:, pl.ds(pl.multiple_of(base, width), width)]
    window[...] = jnp.concatenate([near, jnp.zeros((96, width), F32)], axis=0).T
    own_modes = window[pl.ds(pl.multiple_of(me * own - base, own), own), :].astype(BF16)
    tile = 2 * A

    def trig_step(q):
        part = pl.ds(pl.multiple_of(q * tile, tile), tile)
        turns = dot(own_modes[:, 0:32], pieces_of(meta[:, part]))
        cos, sin = trig_of_turns(turns)
        trig[0:own, part] = cos
        trig[own : 2 * own, part] = sin
        rows = lax.broadcasted_iota(jnp.int32, (A, tile), 0) + me * A
        hit = meta[3:4, part] == rows.astype(F32)
        choose[:, part] = jnp.where(hit, 1.0, 0.0).astype(BF16)

    def trig_range(lo, hi):
        def run(q, carry):
            trig_step(q)
            return carry

        lax.fori_loop(lo, hi, run, 0)

    tiles = atoms // tile
    trig_range(0, tiles // 2)
    grads[1].along_x()
    hidden.along_core()
    trig_range(tiles // 2, tiles * 3 // 4)
    grads[1].along_core()
    trig_range(tiles * 3 // 4, tiles)
    grads[1].finish()

    group = 2 * X * A
    my_rows = pl.ds(pl.multiple_of(me * own, own), own)

    def adjoints(b):
        adjoint = k_scale * dot(trig[...], wide[b, 0:ch, :], 1, 1)
        even, odd = adjoint[0:own], adjoint[own:]
        saved = density[b, my_rows, :].astype(F32)
        factor = filters[b, my_rows, :].astype(F32)
        grad_ref[b] = even * saved[:, 0:ch] + odd * saved[:, ch:]
        ratio = k_scale / a_scale
        weights[0:own, 0:ch] = (saved[:, 0:ch] * factor * ratio).astype(BF16)
        weights[own:, 0:ch] = (saved[:, ch:] * factor * ratio).astype(BF16)
        both = jnp.concatenate([even * factor, odd * factor], axis=0)
        weights[:, ch:] = both.astype(BF16)
        return both.T.astype(BF16)

    def pos_group(b, zt):
        for h in range(X):
            part = pl.ds(pl.multiple_of(zt * group + h * tile, tile), tile)
            mix = dot(weights[...], wide[b, :, part])
            slant = (
                trig[0:own, part].astype(F32) * mix[own:]
                - trig[own:, part].astype(F32) * mix[0:own]
            )
            add = dot(own_modes[:, 0:16], slant.astype(BF16), 0, 0)
            if b == 1:
                pos_sum[:, part] = add
            else:
                pos_sum[:, part] += add

    def order(k):
        return up(z, k + 1, Z)

    def first_copy(zt, rows):
        return remote(
            s1.at[zt, pl.ds(0, rows)],
            r1.at[zt, pl.ds(0, rows)],
            s1_send.at[zt],
            s1_recv.at[zt],
            dev(z, x, 1 - c),
        )

    def second_copy(zt, i, rows):
        k = zt * (X - 1) + i - 1
        return remote(
            s2.at[k, pl.ds(0, rows)],
            r2.at[k, pl.ds(0, rows)],
            s2_send.at[k],
            s2_recv.at[k],
            dev(z, up(x, i, X), c),
        )

    def third_copy(k, rows):
        return remote(
            s3.at[k, pl.ds(0, rows)],
            r3.at[k, pl.ds(0, rows)],
            s3_send.at[k],
            s3_recv.at[k],
            dev(order(k), x, c),
        )

    def block(b, rows):
        turned = adjoints(b)

        def one(k):
            zt = order(k)
            part = pl.ds(pl.multiple_of(zt * group, group), group)
            partial[zt, 0:ch, :] = a_scale * dot(turned, trig[:, part])
            if rows > ch:
                pos_group(b, zt)
                partial[zt, ch:rows, :] = (a_scale * 2.0 * math.pi / BOX) * pos_sum[:, part]
            for i in range(X):
                s1[zt, 0:rows, i * A : (i + 1) * A] = partial[
                    zt, 0:rows, cols(2 * i + 1 - c)
                ].astype(BF16)
            first_copy(zt, rows).start()

        def two(k):
            zt = order(k)
            first_copy(zt, rows).wait_recv()
            for i in range(1, X):
                xt = up(x, i, X)
                s2[zt * (X - 1) + i - 1, 0:rows, :] = (
                    partial[zt, 0:rows, cols(2 * xt + c)]
                    + r1[zt, 0:rows, cols(xt)].astype(F32)
                ).astype(BF16)
                second_copy(zt, i, rows).start()
            acc[zt, 0:rows, :] = partial[zt, 0:rows, cols(2 * x + c)] + r1[
                zt, 0:rows, cols(x)
            ].astype(F32)

        def summed(k):
            zt = order(k)
            total = acc[zt, 0:rows, :]
            for i in range(1, X):
                second_copy(zt, i, rows).wait_recv()
                total = total + r2[zt * (X - 1) + i - 1, 0:rows, :].astype(F32)
            return total

        def three(k):
            s3[k, 0:rows, :] = summed(k).astype(BF16)
            third_copy(k, rows).start()

        repeat(Z, one, 4)
        if rows == ch:
            for k in range(min(2, Z)):
                pos_group(b, order(k))
        repeat(Z, two, 4)
        repeat(Z - 1, three, 4)
        acc[z, 0:rows, :] = summed(Z - 1)

        def last(k):
            third_copy(k, rows).wait_recv()
            acc[z, 0:rows, :] += r3[k, 0:rows, :].astype(F32)

        repeat(Z - 1, last, 4)

        def sent(k):
            first_copy(k, rows).wait_send()
            for i in range(1, X):
                second_copy(k, i, rows).wait_send()

        repeat(Z, sent, 4)
        repeat(Z - 1, lambda k: third_copy(k, rows).wait_send(), 4)

    hidden.finish()
    block(1, ch)
    cot[...] += acc[z, 0:ch, :]
    wide[0, 0:ch, mine] = (cot[...] * slope[0]).astype(BF16)
    grads[0].start()
    repeat(max(Z - 2, 0), lambda k: pos_group(1, order(k + 2)), 4)
    grads[0].along_x()
    grads[0].along_core()
    grads[0].finish()
    block(0, ch + 16)
    fin[0:ch, mine] = (cot[...] + acc[z, 0:ch, :]).astype(BF16)
    fin[ch:, mine] = acc[z, ch:, :].astype(BF16)
    final.start()
    final.along_x()
    final.along_core()
    final.finish()
    feat_ref[...] = dot(choose[...], fin[0:ch, :], 1, 1)
    pos_ref[...] = dot(fin[ch:, :], choose[...], 1, 1)[0:3]
    repeat(n - 1, lambda j: meta_copy(j).wait_send(), 15)


def body(
    dims,
    particle_coordinates,
    integer_lattice_modes,
    hidden_embeddings,
    cached_density_modes,
    spectral_kernels,
    final_embedding_adjoint,
    particle_result_line,
):
    Z, X = dims
    n = Z * X * 2
    blocks, A, ch = hidden_embeddings.shape
    modes = integer_lattice_modes.shape[1]
    own = modes // n
    atoms = n * A
    rows = ch + 16
    chunks = 8
    vmem = pl.BlockSpec(memory_space=pltpu.VMEM)
    hbm = pl.BlockSpec(memory_space=pl.ANY)
    dma = pltpu.SemaphoreType.DMA
    scratch = [
        pltpu.VMEM((blocks, modes, 2 * ch), BF16),
        pltpu.VMEM((blocks, modes, ch), BF16),
        pltpu.VMEM((8, atoms), F32),
        pltpu.VMEM((32, modes), F32),
        pltpu.VMEM((max(own, 128), 128), F32),
        pltpu.VMEM((2 * own, atoms), BF16),
        pltpu.VMEM((blocks, 2 * ch, atoms), BF16),
        pltpu.VMEM((2 * own, 2 * ch), BF16),
        pltpu.VMEM((rows, atoms), BF16),
        pltpu.VMEM((A, atoms), BF16),
        pltpu.VMEM((A, blocks * ch), F32),
        pltpu.VMEM((blocks, ch, A), F32),
        pltpu.VMEM((ch, A), F32),
        pltpu.VMEM((Z, rows, 2 * X * A), F32),
        pltpu.VMEM((16, atoms), F32),
        pltpu.VMEM((Z, rows, A), F32),
        pltpu.VMEM((Z, rows, X * A), BF16),
        pltpu.VMEM((Z, rows, X * A), BF16),
        pltpu.VMEM((Z * (X - 1), rows, A), BF16),
        pltpu.VMEM((Z * (X - 1), rows, A), BF16),
        pltpu.VMEM((Z - 1, rows, A), BF16),
        pltpu.VMEM((Z - 1, rows, A), BF16),
        dma((chunks, 2)),
        dma((n - 1,)),
        dma((n - 1,)),
        dma((n - 1,)),
        dma((n,)),
        dma((n - 1,)),
        dma((n,)),
        dma((Z,)),
        dma((Z,)),
        dma((Z * (X - 1),)),
        dma((Z * (X - 1),)),
        dma((Z - 1,)),
        dma((Z - 1,)),
    ]
    return pl.pallas_call(
        functools.partial(kernel, dims),
        out_shape=(
            jax.ShapeDtypeStruct((A, ch), F32),
            jax.ShapeDtypeStruct((3, A), F32),
            jax.ShapeDtypeStruct((blocks, own, ch), F32),
        ),
        in_specs=[vmem, vmem, vmem, hbm, hbm, vmem, vmem],
        out_specs=(vmem, vmem, vmem),
        scratch_shapes=scratch,
        compiler_params=pltpu.CompilerParams(
            collective_id=0, has_side_effects=True, vmem_limit_bytes=60 * 1024 * 1024
        ),
    )(
        particle_coordinates,
        integer_lattice_modes,
        hidden_embeddings,
        cached_density_modes,
        spectral_kernels,
        final_embedding_adjoint,
        particle_result_line.reshape(1, A),
    )


def chip_grid(mesh):
    chips = mesh.shape[AXIS] // 2
    first = mesh.devices[0]
    inner = 0
    try:
        inner = len({device.coords[0] for device in first})
    except AttributeError:
        pass
    if inner < 2 or chips % inner or chips // inner < 2:
        inner = 2
    return chips // inner, inner


def solution(mesh):
    in_specs = (
        P(None, ("groups", "atoms")),
        P(),
        P(None, ("groups", "atoms"), None),
        P("groups", None, None),
        P(),
        P(("groups", "atoms"), None),
        P(("groups", "atoms")),
    )
    out_specs = (
        P(("groups", "atoms"), None),
        P(None, ("groups", "atoms")),
        P(None, ("groups", "atoms"), None),
    )
    return jax.shard_map(
        functools.partial(body, chip_grid(mesh)),
        mesh=mesh,
        in_specs=in_specs,
        out_specs=out_specs,
        check_vma=False,
    )
```

```python
import functools
import math

import jax
import jax.numpy as jnp
from jax import lax
from jax.experimental import pallas as pl
from jax.experimental.pallas import tpu as pltpu
from jax.sharding import PartitionSpec as P

BOX = 72
AXIS = "atoms"
F32, BF16 = jnp.float32, jnp.bfloat16
COS_TERMS = (0.999999212, -19.7389804, 64.9286585, -85.2716283, 58.7905066, -21.0711085)
SIN_TERMS = (6.28318492, -41.3415893, 81.5999439, -76.6144759, 41.3428894, -12.4712447)


def trig_of_turns(turns):
    part = turns - jnp.round(turns)
    square = part * part
    cos = COS_TERMS[-1]
    sin = SIN_TERMS[-1]
    for a in COS_TERMS[-2::-1]:
        cos = cos * square + a
    for a in SIN_TERMS[-2::-1]:
        sin = sin * square + a
    return cos.astype(BF16), (sin * part).astype(BF16)


def dot(a, b, ca=1, cb=0):
    return lax.dot_general(a, b, (((ca,), (cb,)), ((), ())), preferred_element_type=F32)


def repeat(count, step, most=8):
    if count <= most:
        for i in range(count):
            step(i)
    else:

        def run(i, carry):
            step(i)
            return carry

        lax.fori_loop(0, count, run, 0)


def pieces_of(rows):
    keep = lax.broadcasted_iota(jnp.int32, rows.shape, 0) < 3
    value = jnp.where(keep, rows * (1.0 / BOX), 0.0)
    high = value.astype(BF16).astype(F32)
    rest = value - high
    mid = rest.astype(BF16).astype(F32)
    return jnp.concatenate([high, mid, rest - mid, jnp.zeros_like(rows)], axis=0).astype(BF16)


def kernel(
    dims,
    coords_ref,
    modes_ref,
    hidden_ref,
    density_hbm,
    filter_hbm,
    cot_ref,
    line_ref,
    feat_ref,
    pos_ref,
    grad_ref,
    density,
    filters,
    meta,
    lattice,
    window,
    trig,
    wide,
    weights,
    fin,
    choose,
    message,
    slope,
    cot,
    partial,
    pos_sum,
    acc,
    s1,
    r1,
    s2,
    r2,
    s3,
    r3,
    load_sem,
    meta_send,
    meta_recv,
    hid_send,
    hid_recv,
    gat_send,
    gat_recv,
    s1_send,
    s1_recv,
    s2_send,
    s2_recv,
    s3_send,
    s3_recv,
):
    Z, X = dims
    n = Z * X * 2
    ch = cot_ref.shape[1]
    A = cot_ref.shape[0]
    modes = modes_ref.shape[1]
    own = modes // n
    atoms = n * A
    k_scale = modes ** (-0.5)
    a_scale = atoms ** (-0.5)
    me = lax.axis_index(AXIS)
    c = lax.rem(me, 2)
    x = lax.rem(me // 2, X)
    z = me // (2 * X)
    chunks = load_sem.shape[0]
    step_modes = modes // chunks

    def dev(zz, xx, cc):
        return (zz * X + xx) * 2 + cc

    def up(base, j, size):
        return lax.rem(base + j, size)

    def cols(d):
        return pl.ds(pl.multiple_of(d * A, A), A)

    def remote(src, dst, ssem, rsem, peer):
        return pltpu.make_async_remote_copy(
            src_ref=src,
            dst_ref=dst,
            send_sem=ssem,
            recv_sem=rsem,
            device_id={AXIS: peer},
            device_id_type=pl.DeviceIdType.MESH,
        )

    def loads(q):
        part = pl.ds(pl.multiple_of(q * step_modes, step_modes), step_modes)
        return (
            pltpu.make_async_copy(density_hbm.at[:, part], density.at[:, part], load_sem.at[q, 0]),
            pltpu.make_async_copy(filter_hbm.at[:, part], filters.at[:, part], load_sem.at[q, 1]),
        )

    def start_load(q):
        for copy in loads(q):
            copy.start()

    repeat(chunks, start_load)

    barrier = pltpu.get_barrier_semaphore()

    def greet(j):
        pl.semaphore_signal(
            barrier,
            inc=1,
            device_id={AXIS: up(me, j + 1, n)},
            device_id_type=pl.DeviceIdType.MESH,
        )

    repeat(n - 1, greet, 15)

    mine = cols(me)
    meta[:, mine] = jnp.zeros((8, A), F32)
    meta[0:3, mine] = coords_ref[...]
    meta[3:4, mine] = line_ref[...].astype(F32)
    for b in range(2):
        wide[b, ch : 2 * ch, mine] = hidden_ref[b].astype(F32).T.astype(BF16)
    pl.semaphore_wait(barrier, n - 1)

    def meta_copy(j):
        peer = up(me, j + 1, n)
        return remote(
            meta.at[:, mine], meta.at[:, mine], meta_send.at[j], meta_recv.at[j], peer
        )

    repeat(n - 1, lambda j: meta_copy(j).start(), 15)

    class Gather:
        def __init__(self, view, send, recv):
            self.view, self.send, self.recv = view, send, recv

        def copy(self, d, peer, k):
            return remote(self.view(d), self.view(d), self.send.at[k], self.recv.at[d], peer)

        def arrive(self, d):
            self.copy(d, up(me, 1, n), 0).wait_recv()

        def spread(self, d, j):
            for i in range(1, X):
                self.copy(d, dev(z, up(x, i, X), c), Z - 1 + j * (X - 1) + i - 1).start()
            self.copy(d, dev(z, x, 1 - c), Z - 1 + Z * (X - 1) + j * X).start()

        def start(self):
            repeat(
                Z - 1, lambda j: self.copy(me, dev(up(z, j + 1, Z), x, c), j).start()
            )
            self.spread(me, 0)

        def along_x(self):
            def step(j):
                d = dev(up(z, j + 1, Z), x, c)
                self.arrive(d)
                self.spread(d, j + 1)

            repeat(Z - 1, step)

        def along_core(self):
            def step(j):
                for i in range(1, X):
                    d = dev(up(z, j, Z), up(x, i, X), c)
                    self.arrive(d)
                    self.copy(d, dev(z, x, 1 - c), Z - 1 + Z * (X - 1) + j * X + i).start()

            repeat(Z, step)

        def finish(self):
            def step(j):
                for i in range(X):
                    self.arrive(dev(up(z, j, Z), up(x, i, X), 1 - c))

            repeat(Z, step)
            repeat(n - 1, lambda k: self.copy(me, up(me, 1, n), k).wait_send(), 15)

    hidden = Gather(lambda d: wide.at[:, pl.ds(ch, ch), cols(d)], hid_send, hid_recv)
    grads = [
        Gather(lambda d, b=b: wide.at[b, pl.ds(0, ch), cols(d)], gat_send, gat_recv)
        for b in range(2)
    ]
    final = Gather(lambda d: fin.at[:, cols(d)], gat_send, gat_recv)
    hidden.start()

    eight = jnp.concatenate(
        [modes_ref[...].astype(F32), jnp.zeros((5, modes), F32)], axis=0
    )
    lattice[...] = jnp.concatenate([eight, eight, eight, jnp.zeros_like(eight)], axis=0)
    my_pieces = pieces_of(meta[:, mine])
    message[...] = jnp.zeros_like(message)

    def message_step(q):
        part = pl.ds(pl.multiple_of(q * step_modes, step_modes), step_modes)
        cos, sin = trig_of_turns(dot(my_pieces, lattice[:, part].astype(BF16), 0, 0))
        for copy in loads(q):
            copy.wait()
        even, odd = [], []
        for b in range(2):
            factor = filters[b, part, :]
            even.append(density[b, part, 0:ch] * factor)
            odd.append(density[b, part, ch : 2 * ch] * factor)
        message[...] += dot(cos, jnp.concatenate(even, axis=1)) + dot(
            sin, jnp.concatenate(odd, axis=1)
        )

    repeat(chunks, message_step, 0)

    for b in range(2):
        value = k_scale * message[:, b * ch : (b + 1) * ch]
        logistic = 1.0 / (1.0 + jnp.exp(-value))
        slope[b] = (logistic * (1.0 + value * (1.0 - logistic))).T
    cot[...] = cot_ref[...].astype(F32).T
    wide[1, 0:ch, mine] = (cot[...] * slope[1]).astype(BF16)
    grads[1].start()

    repeat(n - 1, lambda j: meta_copy(j).wait_recv(), 15)
    width = window.shape[0]
    base = (me * own) // width * width
    near = lattice[:, pl.ds(pl.multiple_of(base, width), width)]
    window[...] = jnp.concatenate([near, jnp.zeros((96, width), F32)], axis=0).T
    own_modes = window[pl.ds(pl.multiple_of(me * own - base, own), own), :].astype(BF16)
    tile = 2 * A

    def trig_step(q):
        part = pl.ds(pl.multiple_of(q * tile, tile), tile)
        turns = dot(own_modes[:, 0:32], pieces_of(meta[:, part]))
        cos, sin = trig_of_turns(turns)
        trig[0:own, part] = cos
        trig[own : 2 * own, part] = sin
        rows = lax.broadcasted_iota(jnp.int32, (A, tile), 0) + me * A
        hit = meta[3:4, part] == rows.astype(F32)
        choose[:, part] = jnp.where(hit, 1.0, 0.0).astype(BF16)

    def trig_range(lo, hi):
        def run(q, carry):
            trig_step(q)
            return carry

        lax.fori_loop(lo, hi, run, 0)

    tiles = atoms // tile
    trig_range(0, tiles // 2)
    grads[1].along_x()
    hidden.along_x()
    trig_range(tiles // 2, tiles * 3 // 4)
    grads[1].along_core()
    trig_range(tiles * 3 // 4, tiles)
    grads[1].finish()

    group = 2 * X * A
    my_rows = pl.ds(pl.multiple_of(me * own, own), own)

    def adjoints(b):
        adjoint = k_scale * dot(trig[...], wide[b, 0:ch, :], 1, 1)
        even, odd = adjoint[0:own], adjoint[own:]
        saved = density[b, my_rows, :].astype(F32)
        factor = filters[b, my_rows, :].astype(F32)
        grad_ref[b] = even * saved[:, 0:ch] + odd * saved[:, ch:]
        ratio = k_scale / a_scale
        weights[0:own, 0:ch] = (saved[:, 0:ch] * factor * ratio).astype(BF16)
        weights[own:, 0:ch] = (saved[:, ch:] * factor * ratio).astype(BF16)
        both = jnp.concatenate([even * factor, odd * factor], axis=0)
        weights[:, ch:] = both.astype(BF16)
        return both.T.astype(BF16)

    def pos_group(b, zt):
        for h in range(X):
            part = pl.ds(pl.multiple_of(zt * group + h * tile, tile), tile)
            mix = dot(weights[...], wide[b, :, part])
            slant = (
                trig[0:own, part].astype(F32) * mix[own:]
                - trig[own:, part].astype(F32) * mix[0:own]
            )
            add = dot(own_modes[:, 0:16], slant.astype(BF16), 0, 0)
            if b == 1:
                pos_sum[:, part] = add
            else:
                pos_sum[:, part] += add

    def order(k):
        return up(z, k + 1, Z)

    def first_copy(zt, rows):
        return remote(
            s1.at[zt, pl.ds(0, rows)],
            r1.at[zt, pl.ds(0, rows)],
            s1_send.at[zt],
            s1_recv.at[zt],
            dev(z, x, 1 - c),
        )

    def second_copy(zt, i, rows):
        k = zt * (X - 1) + i - 1
        return remote(
            s2.at[k, pl.ds(0, rows)],
            r2.at[k, pl.ds(0, rows)],
            s2_send.at[k],
            s2_recv.at[k],
            dev(z, up(x, i, X), c),
        )

    def third_copy(k, rows):
        return remote(
            s3.at[k, pl.ds(0, rows)],
            r3.at[k, pl.ds(0, rows)],
            s3_send.at[k],
            s3_recv.at[k],
            dev(order(k), x, c),
        )

    def block(b, rows):
        turned = adjoints(b)

        def one(k):
            zt = order(k)
            part = pl.ds(pl.multiple_of(zt * group, group), group)
            partial[zt, 0:ch, :] = a_scale * dot(turned, trig[:, part])
            if rows > ch:
                pos_group(b, zt)
                partial[zt, ch:rows, :] = (a_scale * 2.0 * math.pi / BOX) * pos_sum[:, part]
            for i in range(X):
                s1[zt, 0:rows, i * A : (i + 1) * A] = partial[
                    zt, 0:rows, cols(2 * i + 1 - c)
                ].astype(BF16)
            first_copy(zt, rows).start()

        def two(k):
            zt = order(k)
            first_copy(zt, rows).wait_recv()
            for i in range(1, X):
                xt = up(x, i, X)
                s2[zt * (X - 1) + i - 1, 0:rows, :] = (
                    partial[zt, 0:rows, cols(2 * xt + c)]
                    + r1[zt, 0:rows, cols(xt)].astype(F32)
                ).astype(BF16)
                second_copy(zt, i, rows).start()
            acc[zt, 0:rows, :] = partial[zt, 0:rows, cols(2 * x + c)] + r1[
                zt, 0:rows, cols(x)
            ].astype(F32)

        def summed(k):
            zt = order(k)
            total = acc[zt, 0:rows, :]
            for i in range(1, X):
                second_copy(zt, i, rows).wait_recv()
                total = total + r2[zt * (X - 1) + i - 1, 0:rows, :].astype(F32)
            return total

        def three(k):
            s3[k, 0:rows, :] = summed(k).astype(BF16)
            third_copy(k, rows).start()

        repeat(Z, one, 4)
        if rows == ch:
            hidden.along_core()
        repeat(Z, two, 4)
        repeat(Z - 1, three, 4)
        acc[z, 0:rows, :] = summed(Z - 1)

        def last(k):
            third_copy(k, rows).wait_recv()
            acc[z, 0:rows, :] += r3[k, 0:rows, :].astype(F32)

        repeat(Z - 1, last, 4)

        def sent(k):
            first_copy(k, rows).wait_send()
            for i in range(1, X):
                second_copy(k, i, rows).wait_send()

        repeat(Z, sent, 4)
        repeat(Z - 1, lambda k: third_copy(k, rows).wait_send(), 4)

    block(1, ch)
    cot[...] += acc[z, 0:ch, :]
    wide[0, 0:ch, mine] = (cot[...] * slope[0]).astype(BF16)
    grads[0].start()
    hidden.finish()
    repeat(Z, lambda k: pos_group(1, order(k)), 4)
    grads[0].along_x()
    grads[0].along_core()
    grads[0].finish()
    block(0, ch + 16)
    fin[0:ch, mine] = (cot[...] + acc[z, 0:ch, :]).astype(BF16)
    fin[ch:, mine] = acc[z, ch:, :].astype(BF16)
    final.start()
    final.along_x()
    final.along_core()
    final.finish()
    feat_ref[...] = dot(choose[...], fin[0:ch, :], 1, 1)
    pos_ref[...] = dot(fin[ch:, :], choose[...], 1, 1)[0:3]
    repeat(n - 1, lambda j: meta_copy(j).wait_send(), 15)


def body(
    dims,
    particle_coordinates,
    integer_lattice_modes,
    hidden_embeddings,
    cached_density_modes,
    spectral_kernels,
    final_embedding_adjoint,
    particle_result_line,
):
    Z, X = dims
    n = Z * X * 2
    blocks, A, ch = hidden_embeddings.shape
    modes = integer_lattice_modes.shape[1]
    own = modes // n
    atoms = n * A
    rows = ch + 16
    chunks = 8
    vmem = pl.BlockSpec(memory_space=pltpu.VMEM)
    hbm = pl.BlockSpec(memory_space=pl.ANY)
    dma = pltpu.SemaphoreType.DMA
    scratch = [
        pltpu.VMEM((blocks, modes, 2 * ch), BF16),
        pltpu.VMEM((blocks, modes, ch), BF16),
        pltpu.VMEM((8, atoms), F32),
        pltpu.VMEM((32, modes), F32),
        pltpu.VMEM((max(own, 128), 128), F32),
        pltpu.VMEM((2 * own, atoms), BF16),
        pltpu.VMEM((blocks, 2 * ch, atoms), BF16),
        pltpu.VMEM((2 * own, 2 * ch), BF16),
        pltpu.VMEM((rows, atoms), BF16),
        pltpu.VMEM((A, atoms), BF16),
        pltpu.VMEM((A, blocks * ch), F32),
        pltpu.VMEM((blocks, ch, A), F32),
        pltpu.VMEM((ch, A), F32),
        pltpu.VMEM((Z, rows, 2 * X * A), F32),
        pltpu.VMEM((16, atoms), F32),
        pltpu.VMEM((Z, rows, A), F32),
        pltpu.VMEM((Z, rows, X * A), BF16),
        pltpu.VMEM((Z, rows, X * A), BF16),
        pltpu.VMEM((Z * (X - 1), rows, A), BF16),
        pltpu.VMEM((Z * (X - 1), rows, A), BF16),
        pltpu.VMEM((Z - 1, rows, A), BF16),
        pltpu.VMEM((Z - 1, rows, A), BF16),
        dma((chunks, 2)),
        dma((n - 1,)),
        dma((n - 1,)),
        dma((n - 1,)),
        dma((n,)),
        dma((n - 1,)),
        dma((n,)),
        dma((Z,)),
        dma((Z,)),
        dma((Z * (X - 1),)),
        dma((Z * (X - 1),)),
        dma((Z - 1,)),
        dma((Z - 1,)),
    ]
    return pl.pallas_call(
        functools.partial(kernel, dims),
        out_shape=(
            jax.ShapeDtypeStruct((A, ch), F32),
            jax.ShapeDtypeStruct((3, A), F32),
            jax.ShapeDtypeStruct((blocks, own, ch), F32),
        ),
        in_specs=[vmem, vmem, vmem, hbm, hbm, vmem, vmem],
        out_specs=(vmem, vmem, vmem),
        scratch_shapes=scratch,
        compiler_params=pltpu.CompilerParams(
            collective_id=0, has_side_effects=True, vmem_limit_bytes=60 * 1024 * 1024
        ),
    )(
        particle_coordinates,
        integer_lattice_modes,
        hidden_embeddings,
        cached_density_modes,
        spectral_kernels,
        final_embedding_adjoint,
        particle_result_line.reshape(1, A),
    )


def chip_grid(mesh):
    chips = mesh.shape[AXIS] // 2
    first = mesh.devices[0]
    inner = 0
    try:
        inner = len({device.coords[0] for device in first})
    except AttributeError:
        pass
    if inner < 2 or chips % inner or chips // inner < 2:
        inner = 2
    return chips // inner, inner


def solution(mesh):
    in_specs = (
        P(None, ("groups", "atoms")),
        P(),
        P(None, ("groups", "atoms"), None),
        P("groups", None, None),
        P(),
        P(("groups", "atoms"), None),
        P(("groups", "atoms")),
    )
    out_specs = (
        P(("groups", "atoms"), None),
        P(None, ("groups", "atoms")),
        P(None, ("groups", "atoms"), None),
    )
    return jax.shard_map(
        functools.partial(body, chip_grid(mesh)),
        mesh=mesh,
        in_specs=in_specs,
        out_specs=out_specs,
        check_vma=False,
    )
```

```python
import functools
import math

import jax
import jax.numpy as jnp
from jax import lax
from jax.experimental import pallas as pl
from jax.experimental.pallas import tpu as pltpu
from jax.sharding import PartitionSpec as P

BOX = 72
AXIS = "atoms"
F32, BF16 = jnp.float32, jnp.bfloat16
COS_TERMS = (0.999999212, -19.7389804, 64.9286585, -85.2716283, 58.7905066, -21.0711085)
SIN_TERMS = (6.28318492, -41.3415893, 81.5999439, -76.6144759, 41.3428894, -12.4712447)


def trig_of_turns(turns):
    part = turns - jnp.round(turns)
    square = part * part
    cos = COS_TERMS[-1]
    sin = SIN_TERMS[-1]
    for a in COS_TERMS[-2::-1]:
        cos = cos * square + a
    for a in SIN_TERMS[-2::-1]:
        sin = sin * square + a
    return cos.astype(BF16), (sin * part).astype(BF16)


def dot(a, b, ca=1, cb=0):
    return lax.dot_general(a, b, (((ca,), (cb,)), ((), ())), preferred_element_type=F32)


def repeat(count, step, most=8):
    if count <= most:
        for i in range(count):
            step(i)
    else:

        def run(i, carry):
            step(i)
            return carry

        lax.fori_loop(0, count, run, 0)


def pieces_of(rows):
    keep = lax.broadcasted_iota(jnp.int32, rows.shape, 0) < 3
    value = jnp.where(keep, rows * (1.0 / BOX), 0.0)
    high = value.astype(BF16).astype(F32)
    rest = value - high
    mid = rest.astype(BF16).astype(F32)
    return jnp.concatenate([high, mid, rest - mid, jnp.zeros_like(rows)], axis=0).astype(BF16)


def kernel(
    dims,
    coords_ref,
    modes_ref,
    hidden_ref,
    density_hbm,
    filter_hbm,
    cot_ref,
    line_ref,
    feat_ref,
    pos_ref,
    grad_ref,
    density,
    filters,
    meta,
    lattice,
    window,
    trig,
    wide,
    weights,
    fin,
    choose,
    message,
    slope,
    cot,
    partial,
    pos_sum,
    acc,
    s1,
    r1,
    s2,
    r2,
    s3,
    r3,
    load_sem,
    meta_send,
    meta_recv,
    hid_send,
    hid_recv,
    gat_send,
    gat_recv,
    s1_send,
    s1_recv,
    s2_send,
    s2_recv,
    s3_send,
    s3_recv,
):
    Z, X = dims
    n = Z * X * 2
    ch = cot_ref.shape[1]
    A = cot_ref.shape[0]
    modes = modes_ref.shape[1]
    own = modes // n
    atoms = n * A
    k_scale = modes ** (-0.5)
    a_scale = atoms ** (-0.5)
    me = lax.axis_index(AXIS)
    c = lax.rem(me, 2)
    x = lax.rem(me // 2, X)
    z = me // (2 * X)
    chunks = load_sem.shape[0]
    step_modes = modes // chunks

    def dev(zz, xx, cc):
        return (zz * X + xx) * 2 + cc

    def up(base, j, size):
        return lax.rem(base + j, size)

    def swap(j):
        if Z & (Z - 1):
            return up(z, j, Z)
        total, bit = 0, 1
        while bit < Z:
            total = total + bit * lax.rem(lax.div(z, bit) + (j // bit) % 2, 2)
            bit *= 2
        return total

    def cols(d):
        return pl.ds(pl.multiple_of(d * A, A), A)

    def remote(src, dst, ssem, rsem, peer):
        return pltpu.make_async_remote_copy(
            src_ref=src,
            dst_ref=dst,
            send_sem=ssem,
            recv_sem=rsem,
            device_id={AXIS: peer},
            device_id_type=pl.DeviceIdType.MESH,
        )

    def loads(q):
        part = pl.ds(pl.multiple_of(q * step_modes, step_modes), step_modes)
        return (
            pltpu.make_async_copy(density_hbm.at[:, part], density.at[:, part], load_sem.at[q, 0]),
            pltpu.make_async_copy(filter_hbm.at[:, part], filters.at[:, part], load_sem.at[q, 1]),
        )

    def start_load(q):
        for copy in loads(q):
            copy.start()

    repeat(chunks, start_load)

    barrier = pltpu.get_barrier_semaphore()

    def greet(j):
        pl.semaphore_signal(
            barrier,
            inc=1,
            device_id={AXIS: up(me, j + 1, n)},
            device_id_type=pl.DeviceIdType.MESH,
        )

    repeat(n - 1, greet, 15)

    mine = cols(me)
    meta[:, mine] = jnp.zeros((8, A), F32)
    meta[0:3, mine] = coords_ref[...]
    meta[3:4, mine] = line_ref[...].astype(F32)
    for b in range(2):
        wide[b, ch : 2 * ch, mine] = hidden_ref[b].astype(F32).T.astype(BF16)
    pl.semaphore_wait(barrier, n - 1)

    def meta_copy(j):
        peer = up(me, j + 1, n)
        return remote(
            meta.at[:, mine], meta.at[:, mine], meta_send.at[j], meta_recv.at[j], peer
        )

    repeat(n - 1, lambda j: meta_copy(j).start(), 15)

    class Gather:
        def __init__(self, view, send, recv):
            self.view, self.send, self.recv = view, send, recv

        def copy(self, d, peer, k):
            return remote(self.view(d), self.view(d), self.send.at[k], self.recv.at[d], peer)

        def arrive(self, d):
            self.copy(d, up(me, 1, n), 0).wait_recv()

        def spread(self, d, j):
            for i in range(1, X):
                self.copy(d, dev(z, up(x, i, X), c), Z - 1 + j * (X - 1) + i - 1).start()
            self.copy(d, dev(z, x, 1 - c), Z - 1 + Z * (X - 1) + j * X).start()

        def start(self):
            repeat(
                Z - 1, lambda j: self.copy(me, dev(swap(j + 1), x, c), j).start()
            )
            self.spread(me, 0)

        def along_x(self):
            def step(j):
                d = dev(swap(j + 1), x, c)
                self.arrive(d)
                self.spread(d, j + 1)

            repeat(Z - 1, step)

        def along_core(self):
            def step(j):
                for i in range(1, X):
                    d = dev(swap(j), up(x, i, X), c)
                    self.arrive(d)
                    self.copy(d, dev(z, x, 1 - c), Z - 1 + Z * (X - 1) + j * X + i).start()

            repeat(Z, step)

        def finish(self):
            def step(j):
                for i in range(X):
                    self.arrive(dev(swap(j), up(x, i, X), 1 - c))

            repeat(Z, step)
            repeat(n - 1, lambda k: self.copy(me, up(me, 1, n), k).wait_send(), 15)

    hidden = Gather(lambda d: wide.at[:, pl.ds(ch, ch), cols(d)], hid_send, hid_recv)
    grads = [
        Gather(lambda d, b=b: wide.at[b, pl.ds(0, ch), cols(d)], gat_send, gat_recv)
        for b in range(2)
    ]
    final = Gather(lambda d: fin.at[:, cols(d)], gat_send, gat_recv)
    hidden.start()

    eight = jnp.concatenate(
        [modes_ref[...].astype(F32), jnp.zeros((5, modes), F32)], axis=0
    )
    lattice[...] = jnp.concatenate([eight, eight, eight, jnp.zeros_like(eight)], axis=0)
    my_pieces = pieces_of(meta[:, mine])
    message[...] = jnp.zeros_like(message)

    def message_step(q):
        part = pl.ds(pl.multiple_of(q * step_modes, step_modes), step_modes)
        cos, sin = trig_of_turns(dot(my_pieces, lattice[:, part].astype(BF16), 0, 0))
        for copy in loads(q):
            copy.wait()
        even, odd = [], []
        for b in range(2):
            factor = filters[b, part, :]
            even.append(density[b, part, 0:ch] * factor)
            odd.append(density[b, part, ch : 2 * ch] * factor)
        message[...] += dot(cos, jnp.concatenate(even, axis=1)) + dot(
            sin, jnp.concatenate(odd, axis=1)
        )

    repeat(chunks, message_step, 0)

    for b in range(2):
        value = k_scale * message[:, b * ch : (b + 1) * ch]
        logistic = 1.0 / (1.0 + jnp.exp(-value))
        slope[b] = (logistic * (1.0 + value * (1.0 - logistic))).T
    cot[...] = cot_ref[...].astype(F32).T
    wide[1, 0:ch, mine] = (cot[...] * slope[1]).astype(BF16)
    grads[1].start()

    repeat(n - 1, lambda j: meta_copy(j).wait_recv(), 15)
    width = window.shape[0]
    base = (me * own) // width * width
    near = lattice[:, pl.ds(pl.multiple_of(base, width), width)]
    window[...] = jnp.concatenate([near, jnp.zeros((96, width), F32)], axis=0).T
    own_modes = window[pl.ds(pl.multiple_of(me * own - base, own), own), :].astype(BF16)
    tile = 2 * A

    def trig_step(q):
        part = pl.ds(pl.multiple_of(q * tile, tile), tile)
        turns = dot(own_modes[:, 0:32], pieces_of(meta[:, part]))
        cos, sin = trig_of_turns(turns)
        trig[0:own, part] = cos
        trig[own : 2 * own, part] = sin
        rows = lax.broadcasted_iota(jnp.int32, (A, tile), 0) + me * A
        hit = meta[3:4, part] == rows.astype(F32)
        choose[:, part] = jnp.where(hit, 1.0, 0.0).astype(BF16)

    def trig_range(lo, hi):
        def run(q, carry):
            trig_step(q)
            return carry

        lax.fori_loop(lo, hi, run, 0)

    tiles = atoms // tile
    trig_range(0, tiles // 2)
    grads[1].along_x()
    hidden.along_x()
    trig_range(tiles // 2, tiles * 3 // 4)
    grads[1].along_core()
    trig_range(tiles * 3 // 4, tiles)
    grads[1].finish()

    group = 2 * X * A
    my_rows = pl.ds(pl.multiple_of(me * own, own), own)

    def adjoints(b):
        adjoint = k_scale * dot(trig[...], wide[b, 0:ch, :], 1, 1)
        even, odd = adjoint[0:own], adjoint[own:]
        saved = density[b, my_rows, :].astype(F32)
        factor = filters[b, my_rows, :].astype(F32)
        grad_ref[b] = even * saved[:, 0:ch] + odd * saved[:, ch:]
        ratio = k_scale / a_scale
        weights[0:own, 0:ch] = (saved[:, 0:ch] * factor * ratio).astype(BF16)
        weights[own:, 0:ch] = (saved[:, ch:] * factor * ratio).astype(BF16)
        both = jnp.concatenate([even * factor, odd * factor], axis=0)
        weights[:, ch:] = both.astype(BF16)
        return both.T.astype(BF16)

    def pos_group(b, zt):
        for h in range(X):
            part = pl.ds(pl.multiple_of(zt * group + h * tile, tile), tile)
            mix = dot(weights[...], wide[b, :, part])
            slant = (
                trig[0:own, part].astype(F32) * mix[own:]
                - trig[own:, part].astype(F32) * mix[0:own]
            )
            add = dot(own_modes[:, 0:16], slant.astype(BF16), 0, 0)
            if b == 1:
                pos_sum[:, part] = add
            else:
                pos_sum[:, part] += add

    def order(k):
        return up(z, k + 1, Z) if Z & (Z - 1) else swap(Z - 1 - k)

    def first_copy(zt, rows):
        return remote(
            s1.at[zt, pl.ds(0, rows)],
            r1.at[zt, pl.ds(0, rows)],
            s1_send.at[zt],
            s1_recv.at[zt],
            dev(z, x, 1 - c),
        )

    def second_copy(zt, i, rows):
        k = zt * (X - 1) + i - 1
        return remote(
            s2.at[k, pl.ds(0, rows)],
            r2.at[k, pl.ds(0, rows)],
            s2_send.at[k],
            s2_recv.at[k],
            dev(z, up(x, i, X), c),
        )

    def third_copy(k, rows):
        return remote(
            s3.at[k, pl.ds(0, rows)],
            r3.at[k, pl.ds(0, rows)],
            s3_send.at[k],
            s3_recv.at[k],
            dev(order(k), x, c),
        )

    def block(b, rows):
        turned = adjoints(b)

        def one(k):
            zt = order(k)
            part = pl.ds(pl.multiple_of(zt * group, group), group)
            partial[zt, 0:ch, :] = a_scale * dot(turned, trig[:, part])
            if rows > ch:
                pos_group(b, zt)
                partial[zt, ch:rows, :] = (a_scale * 2.0 * math.pi / BOX) * pos_sum[:, part]
            for i in range(X):
                s1[zt, 0:rows, i * A : (i + 1) * A] = partial[
                    zt, 0:rows, cols(2 * i + 1 - c)
                ].astype(BF16)
            first_copy(zt, rows).start()

        def two(k):
            zt = order(k)
            first_copy(zt, rows).wait_recv()
            for i in range(1, X):
                xt = up(x, i, X)
                s2[zt * (X - 1) + i - 1, 0:rows, :] = (
                    partial[zt, 0:rows, cols(2 * xt + c)]
                    + r1[zt, 0:rows, cols(xt)].astype(F32)
                ).astype(BF16)
                second_copy(zt, i, rows).start()
            acc[zt, 0:rows, :] = partial[zt, 0:rows, cols(2 * x + c)] + r1[
                zt, 0:rows, cols(x)
            ].astype(F32)

        def summed(k):
            zt = order(k)
            total = acc[zt, 0:rows, :]
            for i in range(1, X):
                second_copy(zt, i, rows).wait_recv()
                total = total + r2[zt * (X - 1) + i - 1, 0:rows, :].astype(F32)
            return total

        def three(k):
            s3[k, 0:rows, :] = summed(k).astype(BF16)
            third_copy(k, rows).start()

        repeat(Z, one, 4)
        if rows == ch:
            hidden.along_core()
        repeat(Z, two, 4)
        repeat(Z - 1, three, 4)
        acc[z, 0:rows, :] = summed(Z - 1)

        def last(k):
            third_copy(k, rows).wait_recv()
            acc[z, 0:rows, :] += r3[k, 0:rows, :].astype(F32)

        repeat(Z - 1, last, 4)

        def sent(k):
            first_copy(k, rows).wait_send()
            for i in range(1, X):
                second_copy(k, i, rows).wait_send()

        repeat(Z, sent, 4)
        repeat(Z - 1, lambda k: third_copy(k, rows).wait_send(), 4)

    block(1, ch)
    cot[...] += acc[z, 0:ch, :]
    wide[0, 0:ch, mine] = (cot[...] * slope[0]).astype(BF16)
    grads[0].start()
    hidden.finish()
    repeat(Z, lambda k: pos_group(1, order(k)), 4)
    grads[0].along_x()
    grads[0].along_core()
    grads[0].finish()
    block(0, ch + 16)
    fin[0:ch, mine] = (cot[...] + acc[z, 0:ch, :]).astype(BF16)
    fin[ch:, mine] = acc[z, ch:, :].astype(BF16)
    final.start()
    final.along_x()
    final.along_core()
    final.finish()
    feat_ref[...] = dot(choose[...], fin[0:ch, :], 1, 1)
    pos_ref[...] = dot(fin[ch:, :], choose[...], 1, 1)[0:3]
    repeat(n - 1, lambda j: meta_copy(j).wait_send(), 15)


def body(
    dims,
    particle_coordinates,
    integer_lattice_modes,
    hidden_embeddings,
    cached_density_modes,
    spectral_kernels,
    final_embedding_adjoint,
    particle_result_line,
):
    Z, X = dims
    n = Z * X * 2
    blocks, A, ch = hidden_embeddings.shape
    modes = integer_lattice_modes.shape[1]
    own = modes // n
    atoms = n * A
    rows = ch + 16
    chunks = 8
    vmem = pl.BlockSpec(memory_space=pltpu.VMEM)
    hbm = pl.BlockSpec(memory_space=pl.ANY)
    dma = pltpu.SemaphoreType.DMA
    scratch = [
        pltpu.VMEM((blocks, modes, 2 * ch), BF16),
        pltpu.VMEM((blocks, modes, ch), BF16),
        pltpu.VMEM((8, atoms), F32),
        pltpu.VMEM((32, modes), F32),
        pltpu.VMEM((max(own, 128), 128), F32),
        pltpu.VMEM((2 * own, atoms), BF16),
        pltpu.VMEM((blocks, 2 * ch, atoms), BF16),
        pltpu.VMEM((2 * own, 2 * ch), BF16),
        pltpu.VMEM((rows, atoms), BF16),
        pltpu.VMEM((A, atoms), BF16),
        pltpu.VMEM((A, blocks * ch), F32),
        pltpu.VMEM((blocks, ch, A), F32),
        pltpu.VMEM((ch, A), F32),
        pltpu.VMEM((Z, rows, 2 * X * A), F32),
        pltpu.VMEM((16, atoms), F32),
        pltpu.VMEM((Z, rows, A), F32),
        pltpu.VMEM((Z, rows, X * A), BF16),
        pltpu.VMEM((Z, rows, X * A), BF16),
        pltpu.VMEM((Z * (X - 1), rows, A), BF16),
        pltpu.VMEM((Z * (X - 1), rows, A), BF16),
        pltpu.VMEM((Z - 1, rows, A), BF16),
        pltpu.VMEM((Z - 1, rows, A), BF16),
        dma((chunks, 2)),
        dma((n - 1,)),
        dma((n - 1,)),
        dma((n - 1,)),
        dma((n,)),
        dma((n - 1,)),
        dma((n,)),
        dma((Z,)),
        dma((Z,)),
        dma((Z * (X - 1),)),
        dma((Z * (X - 1),)),
        dma((Z - 1,)),
        dma((Z - 1,)),
    ]
    return pl.pallas_call(
        functools.partial(kernel, dims),
        out_shape=(
            jax.ShapeDtypeStruct((A, ch), F32),
            jax.ShapeDtypeStruct((3, A), F32),
            jax.ShapeDtypeStruct((blocks, own, ch), F32),
        ),
        in_specs=[vmem, vmem, vmem, hbm, hbm, vmem, vmem],
        out_specs=(vmem, vmem, vmem),
        scratch_shapes=scratch,
        compiler_params=pltpu.CompilerParams(
            collective_id=0, has_side_effects=True, vmem_limit_bytes=60 * 1024 * 1024
        ),
    )(
        particle_coordinates,
        integer_lattice_modes,
        hidden_embeddings,
        cached_density_modes,
        spectral_kernels,
        final_embedding_adjoint,
        particle_result_line.reshape(1, A),
    )


def chip_grid(mesh):
    chips = mesh.shape[AXIS] // 2
    first = mesh.devices[0]
    inner = 0
    try:
        inner = len({device.coords[0] for device in first})
    except AttributeError:
        pass
    if inner < 2 or chips % inner or chips // inner < 2:
        inner = 2
    return chips // inner, inner


def solution(mesh):
    in_specs = (
        P(None, ("groups", "atoms")),
        P(),
        P(None, ("groups", "atoms"), None),
        P("groups", None, None),
        P(),
        P(("groups", "atoms"), None),
        P(("groups", "atoms")),
    )
    out_specs = (
        P(("groups", "atoms"), None),
        P(None, ("groups", "atoms")),
        P(None, ("groups", "atoms"), None),
    )
    return jax.shard_map(
        functools.partial(body, chip_grid(mesh)),
        mesh=mesh,
        in_specs=in_specs,
        out_specs=out_specs,
        check_vma=False,
    )
```

```python
import functools
import math

import jax
import jax.numpy as jnp
from jax import lax
from jax.experimental import pallas as pl
from jax.experimental.pallas import tpu as pltpu
from jax.sharding import PartitionSpec as P

BOX = 72
AXIS = "atoms"
F32, BF16 = jnp.float32, jnp.bfloat16
COS_TERMS = (0.999999212, -19.7389804, 64.9286585, -85.2716283, 58.7905066, -21.0711085)
SIN_TERMS = (6.28318492, -41.3415893, 81.5999439, -76.6144759, 41.3428894, -12.4712447)


def trig_of_turns(turns):
    part = turns - jnp.round(turns)
    square = part * part
    cos = COS_TERMS[-1]
    sin = SIN_TERMS[-1]
    for a in COS_TERMS[-2::-1]:
        cos = cos * square + a
    for a in SIN_TERMS[-2::-1]:
        sin = sin * square + a
    return cos.astype(BF16), (sin * part).astype(BF16)


def dot(a, b, ca=1, cb=0):
    return lax.dot_general(a, b, (((ca,), (cb,)), ((), ())), preferred_element_type=F32)


def repeat(count, step, most=8):
    if count <= most:
        for i in range(count):
            step(i)
    else:

        def run(i, carry):
            step(i)
            return carry

        lax.fori_loop(0, count, run, 0)


def pieces_of(rows):
    keep = lax.broadcasted_iota(jnp.int32, rows.shape, 0) < 3
    value = jnp.where(keep, rows * (1.0 / BOX), 0.0)
    high = value.astype(BF16).astype(F32)
    rest = value - high
    mid = rest.astype(BF16).astype(F32)
    return jnp.concatenate([high, mid, rest - mid, jnp.zeros_like(rows)], axis=0).astype(BF16)


def kernel(
    dims,
    coords_ref,
    modes_ref,
    hidden_ref,
    density_hbm,
    filter_hbm,
    cot_ref,
    line_ref,
    feat_ref,
    pos_ref,
    grad_ref,
    density,
    filters,
    meta,
    lattice,
    window,
    trig,
    wide,
    weights,
    fin,
    choose,
    message,
    slope,
    cot,
    partial,
    pos_sum,
    acc,
    s1,
    r1,
    s2,
    r2,
    s3,
    r3,
    load_sem,
    meta_send,
    meta_recv,
    hid_send,
    hid_recv,
    gat_send,
    gat_recv,
    s1_send,
    s1_recv,
    s2_send,
    s2_recv,
    s3_send,
    s3_recv,
):
    Z, X = dims
    n = Z * X * 2
    ch = cot_ref.shape[1]
    A = cot_ref.shape[0]
    modes = modes_ref.shape[1]
    own = modes // n
    atoms = n * A
    k_scale = modes ** (-0.5)
    a_scale = atoms ** (-0.5)
    me = lax.axis_index(AXIS)
    c = lax.rem(me, 2)
    x = lax.rem(me // 2, X)
    z = me // (2 * X)
    chunks = load_sem.shape[0]
    step_modes = modes // chunks

    def dev(zz, xx, cc):
        return (zz * X + xx) * 2 + cc

    def up(base, j, size):
        return lax.rem(base + j, size)

    def swap(j):
        if Z & (Z - 1):
            return up(z, j, Z)
        total, bit = 0, 1
        while bit < Z:
            total = total + bit * lax.rem(lax.div(z, bit) + (j // bit) % 2, 2)
            bit *= 2
        return total

    def cols(d):
        return pl.ds(pl.multiple_of(d * A, A), A)

    def remote(src, dst, ssem, rsem, peer):
        return pltpu.make_async_remote_copy(
            src_ref=src,
            dst_ref=dst,
            send_sem=ssem,
            recv_sem=rsem,
            device_id={AXIS: peer},
            device_id_type=pl.DeviceIdType.MESH,
        )

    def loads(q):
        part = pl.ds(pl.multiple_of(q * step_modes, step_modes), step_modes)
        return (
            pltpu.make_async_copy(density_hbm.at[:, part], density.at[:, part], load_sem.at[q, 0]),
            pltpu.make_async_copy(filter_hbm.at[:, part], filters.at[:, part], load_sem.at[q, 1]),
        )

    def start_load(q):
        for copy in loads(q):
            copy.start()

    repeat(chunks, start_load)

    barrier = pltpu.get_barrier_semaphore()

    def greet(j):
        pl.semaphore_signal(
            barrier,
            inc=1,
            device_id={AXIS: up(me, j + 1, n)},
            device_id_type=pl.DeviceIdType.MESH,
        )

    repeat(n - 1, greet, 15)

    mine = cols(me)
    meta[:, mine] = jnp.zeros((8, A), F32)
    meta[0:3, mine] = coords_ref[...]
    meta[3:4, mine] = line_ref[...].astype(F32)
    for b in range(2):
        wide[b, ch : 2 * ch, mine] = hidden_ref[b].astype(F32).T.astype(BF16)
    pl.semaphore_wait(barrier, n - 1)

    def meta_copy(j):
        peer = up(me, j + 1, n)
        return remote(
            meta.at[:, mine], meta.at[:, mine], meta_send.at[j], meta_recv.at[j], peer
        )

    repeat(n - 1, lambda j: meta_copy(j).start(), 15)

    class Gather:
        def __init__(self, view, send, recv):
            self.view, self.send, self.recv = view, send, recv

        def copy(self, d, peer, k):
            return remote(self.view(d), self.view(d), self.send.at[k], self.recv.at[d], peer)

        def arrive(self, d):
            self.copy(d, up(me, 1, n), 0).wait_recv()

        def spread(self, d, j):
            for i in range(1, X):
                self.copy(d, dev(z, up(x, i, X), c), Z - 1 + j * (X - 1) + i - 1).start()
            self.copy(d, dev(z, x, 1 - c), Z - 1 + Z * (X - 1) + j * X).start()

        def start(self):
            repeat(
                Z - 1, lambda j: self.copy(me, dev(swap(j + 1), x, c), j).start()
            )
            self.spread(me, 0)

        def along_x(self):
            def step(j):
                d = dev(swap(j + 1), x, c)
                self.arrive(d)
                self.spread(d, j + 1)

            repeat(Z - 1, step)

        def along_core(self):
            def step(j):
                for i in range(1, X):
                    d = dev(swap(j), up(x, i, X), c)
                    self.arrive(d)
                    self.copy(d, dev(z, x, 1 - c), Z - 1 + Z * (X - 1) + j * X + i).start()

            repeat(Z, step)

        def finish(self):
            def step(j):
                for i in range(X):
                    self.arrive(dev(swap(j), up(x, i, X), 1 - c))

            repeat(Z, step)
            repeat(n - 1, lambda k: self.copy(me, up(me, 1, n), k).wait_send(), 15)

    hidden = Gather(lambda d: wide.at[:, pl.ds(ch, ch), cols(d)], hid_send, hid_recv)
    grads = [
        Gather(lambda d, b=b: wide.at[b, pl.ds(0, ch), cols(d)], gat_send, gat_recv)
        for b in range(2)
    ]
    final = Gather(lambda d: fin.at[:, cols(d)], gat_send, gat_recv)
    hidden.start()

    eight = jnp.concatenate(
        [modes_ref[...].astype(F32), jnp.zeros((5, modes), F32)], axis=0
    )
    lattice[...] = jnp.concatenate([eight, eight, eight, jnp.zeros_like(eight)], axis=0)
    my_pieces = pieces_of(meta[:, mine])
    message[...] = jnp.zeros_like(message)

    def message_step(q):
        part = pl.ds(pl.multiple_of(q * step_modes, step_modes), step_modes)
        cos, sin = trig_of_turns(dot(my_pieces, lattice[:, part].astype(BF16), 0, 0))
        for copy in loads(q):
            copy.wait()
        even, odd = [], []
        for b in range(2):
            factor = filters[b, part, :]
            even.append(density[b, part, 0:ch] * factor)
            odd.append(density[b, part, ch : 2 * ch] * factor)
        message[...] += dot(cos, jnp.concatenate(even, axis=1)) + dot(
            sin, jnp.concatenate(odd, axis=1)
        )

    repeat(chunks, message_step, 0)

    for b in range(2):
        value = k_scale * message[:, b * ch : (b + 1) * ch]
        logistic = 1.0 / (1.0 + jnp.exp(-value))
        slope[b] = (logistic * (1.0 + value * (1.0 - logistic))).T
    cot[...] = cot_ref[...].astype(F32).T
    wide[1, 0:ch, mine] = (cot[...] * slope[1]).astype(BF16)
    grads[1].start()

    repeat(n - 1, lambda j: meta_copy(j).wait_recv(), 15)
    width = window.shape[0]
    base = (me * own) // width * width
    near = lattice[:, pl.ds(pl.multiple_of(base, width), width)]
    window[...] = jnp.concatenate([near, jnp.zeros((96, width), F32)], axis=0).T
    own_modes = window[pl.ds(pl.multiple_of(me * own - base, own), own), :].astype(BF16)
    tile = 2 * A

    def trig_step(q):
        part = pl.ds(pl.multiple_of(q * tile, tile), tile)
        turns = dot(own_modes[:, 0:32], pieces_of(meta[:, part]))
        cos, sin = trig_of_turns(turns)
        trig[0:own, part] = cos
        trig[own : 2 * own, part] = sin
        rows = lax.broadcasted_iota(jnp.int32, (A, tile), 0) + me * A
        hit = meta[3:4, part] == rows.astype(F32)
        choose[:, part] = jnp.where(hit, 1.0, 0.0).astype(BF16)

    def trig_range(lo, hi):
        def run(q, carry):
            trig_step(q)
            return carry

        lax.fori_loop(lo, hi, run, 0)

    tiles = atoms // tile
    trig_range(0, tiles // 2)
    grads[1].along_x()
    hidden.along_x()
    trig_range(tiles // 2, tiles * 3 // 4)
    grads[1].along_core()
    trig_range(tiles * 3 // 4, tiles)
    grads[1].finish()

    group = 2 * X * A
    my_rows = pl.ds(pl.multiple_of(me * own, own), own)

    def adjoints(b):
        adjoint = k_scale * dot(trig[...], wide[b, 0:ch, :], 1, 1)
        even, odd = adjoint[0:own], adjoint[own:]
        saved = density[b, my_rows, :].astype(F32)
        factor = filters[b, my_rows, :].astype(F32)
        grad_ref[b] = even * saved[:, 0:ch] + odd * saved[:, ch:]
        ratio = k_scale / a_scale
        weights[0:own, 0:ch] = (saved[:, 0:ch] * factor * ratio).astype(BF16)
        weights[own:, 0:ch] = (saved[:, ch:] * factor * ratio).astype(BF16)
        both = jnp.concatenate([even * factor, odd * factor], axis=0)
        weights[:, ch:] = both.astype(BF16)
        return both.T.astype(BF16)

    def pos_group(b, zt):
        for h in range(X):
            part = pl.ds(pl.multiple_of(zt * group + h * tile, tile), tile)
            mix = dot(weights[...], wide[b, :, part])
            slant = (
                trig[0:own, part].astype(F32) * mix[own:]
                - trig[own:, part].astype(F32) * mix[0:own]
            )
            add = dot(own_modes[:, 0:16], slant.astype(BF16), 0, 0)
            if b == 1:
                pos_sum[:, part] = add
            else:
                pos_sum[:, part] += add

    def order(k):
        return up(z, k + 1, Z) if Z & (Z - 1) else swap(Z - 1 - k)

    def first_copy(zt, rows):
        return remote(
            s1.at[zt, pl.ds(0, rows)],
            r1.at[zt, pl.ds(0, rows)],
            s1_send.at[zt],
            s1_recv.at[zt],
            dev(z, x, 1 - c),
        )

    def second_copy(zt, i, rows):
        k = zt * (X - 1) + i - 1
        return remote(
            s2.at[k, pl.ds(0, rows)],
            r2.at[k, pl.ds(0, rows)],
            s2_send.at[k],
            s2_recv.at[k],
            dev(z, up(x, i, X), c),
        )

    def third_copy(k, rows):
        return remote(
            s3.at[k, pl.ds(0, rows)],
            r3.at[k, pl.ds(0, rows)],
            s3_send.at[k],
            s3_recv.at[k],
            dev(order(k), x, c),
        )

    def block(b, rows):
        turned = adjoints(b)

        def one(k):
            zt = order(k)
            part = pl.ds(pl.multiple_of(zt * group, group), group)
            partial[zt, 0:ch, :] = a_scale * dot(turned, trig[:, part])
            if rows > ch:
                pos_group(b, zt)
                partial[zt, ch:rows, :] = (a_scale * 2.0 * math.pi / BOX) * pos_sum[:, part]
            for i in range(X):
                s1[zt, 0:rows, i * A : (i + 1) * A] = partial[
                    zt, 0:rows, cols(2 * i + 1 - c)
                ].astype(BF16)
            first_copy(zt, rows).start()

        def two(k):
            zt = order(k)
            first_copy(zt, rows).wait_recv()
            for i in range(1, X):
                xt = up(x, i, X)
                s2[zt * (X - 1) + i - 1, 0:rows, :] = (
                    partial[zt, 0:rows, cols(2 * xt + c)]
                    + r1[zt, 0:rows, cols(xt)].astype(F32)
                ).astype(BF16)
                second_copy(zt, i, rows).start()
            acc[zt, 0:rows, :] = partial[zt, 0:rows, cols(2 * x + c)] + r1[
                zt, 0:rows, cols(x)
            ].astype(F32)

        def summed(k):
            zt = order(k)
            total = acc[zt, 0:rows, :]
            for i in range(1, X):
                second_copy(zt, i, rows).wait_recv()
                total = total + r2[zt * (X - 1) + i - 1, 0:rows, :].astype(F32)
            return total

        def three(k):
            s3[k, 0:rows, :] = summed(k).astype(BF16)
            third_copy(k, rows).start()

        repeat(Z, one, 4)
        if rows == ch:
            hidden.along_core()
        two(0)

        def both(k):
            two(k + 1)
            three(k)

        repeat(Z - 1, both, 4)
        acc[z, 0:rows, :] = summed(Z - 1)

        def last(k):
            third_copy(k, rows).wait_recv()
            acc[z, 0:rows, :] += r3[k, 0:rows, :].astype(F32)

        repeat(Z - 1, last, 4)

        def sent(k):
            first_copy(k, rows).wait_send()
            for i in range(1, X):
                second_copy(k, i, rows).wait_send()

        repeat(Z, sent, 4)
        repeat(Z - 1, lambda k: third_copy(k, rows).wait_send(), 4)

    block(1, ch)
    cot[...] += acc[z, 0:ch, :]
    wide[0, 0:ch, mine] = (cot[...] * slope[0]).astype(BF16)
    grads[0].start()
    hidden.finish()
    repeat(Z, lambda k: pos_group(1, order(k)), 4)
    grads[0].along_x()
    grads[0].along_core()
    grads[0].finish()
    block(0, ch + 16)
    fin[0:ch, mine] = (cot[...] + acc[z, 0:ch, :]).astype(BF16)
    fin[ch:, mine] = acc[z, ch:, :].astype(BF16)
    final.start()
    final.along_x()
    final.along_core()
    final.finish()
    feat_ref[...] = dot(choose[...], fin[0:ch, :], 1, 1)
    pos_ref[...] = dot(fin[ch:, :], choose[...], 1, 1)[0:3]
    repeat(n - 1, lambda j: meta_copy(j).wait_send(), 15)


def body(
    dims,
    particle_coordinates,
    integer_lattice_modes,
    hidden_embeddings,
    cached_density_modes,
    spectral_kernels,
    final_embedding_adjoint,
    particle_result_line,
):
    Z, X = dims
    n = Z * X * 2
    blocks, A, ch = hidden_embeddings.shape
    modes = integer_lattice_modes.shape[1]
    own = modes // n
    atoms = n * A
    rows = ch + 16
    chunks = 8
    vmem = pl.BlockSpec(memory_space=pltpu.VMEM)
    hbm = pl.BlockSpec(memory_space=pl.ANY)
    dma = pltpu.SemaphoreType.DMA
    scratch = [
        pltpu.VMEM((blocks, modes, 2 * ch), BF16),
        pltpu.VMEM((blocks, modes, ch), BF16),
        pltpu.VMEM((8, atoms), F32),
        pltpu.VMEM((32, modes), F32),
        pltpu.VMEM((max(own, 128), 128), F32),
        pltpu.VMEM((2 * own, atoms), BF16),
        pltpu.VMEM((blocks, 2 * ch, atoms), BF16),
        pltpu.VMEM((2 * own, 2 * ch), BF16),
        pltpu.VMEM((rows, atoms), BF16),
        pltpu.VMEM((A, atoms), BF16),
        pltpu.VMEM((A, blocks * ch), F32),
        pltpu.VMEM((blocks, ch, A), F32),
        pltpu.VMEM((ch, A), F32),
        pltpu.VMEM((Z, rows, 2 * X * A), F32),
        pltpu.VMEM((16, atoms), F32),
        pltpu.VMEM((Z, rows, A), F32),
        pltpu.VMEM((Z, rows, X * A), BF16),
        pltpu.VMEM((Z, rows, X * A), BF16),
        pltpu.VMEM((Z * (X - 1), rows, A), BF16),
        pltpu.VMEM((Z * (X - 1), rows, A), BF16),
        pltpu.VMEM((Z - 1, rows, A), BF16),
        pltpu.VMEM((Z - 1, rows, A), BF16),
        dma((chunks, 2)),
        dma((n - 1,)),
        dma((n - 1,)),
        dma((n - 1,)),
        dma((n,)),
        dma((n - 1,)),
        dma((n,)),
        dma((Z,)),
        dma((Z,)),
        dma((Z * (X - 1),)),
        dma((Z * (X - 1),)),
        dma((Z - 1,)),
        dma((Z - 1,)),
    ]
    return pl.pallas_call(
        functools.partial(kernel, dims),
        out_shape=(
            jax.ShapeDtypeStruct((A, ch), F32),
            jax.ShapeDtypeStruct((3, A), F32),
            jax.ShapeDtypeStruct((blocks, own, ch), F32),
        ),
        in_specs=[vmem, vmem, vmem, hbm, hbm, vmem, vmem],
        out_specs=(vmem, vmem, vmem),
        scratch_shapes=scratch,
        compiler_params=pltpu.CompilerParams(
            collective_id=0, has_side_effects=True, vmem_limit_bytes=60 * 1024 * 1024
        ),
    )(
        particle_coordinates,
        integer_lattice_modes,
        hidden_embeddings,
        cached_density_modes,
        spectral_kernels,
        final_embedding_adjoint,
        particle_result_line.reshape(1, A),
    )


def chip_grid(mesh):
    chips = mesh.shape[AXIS] // 2
    first = mesh.devices[0]
    inner = 0
    try:
        inner = len({device.coords[0] for device in first})
    except AttributeError:
        pass
    if inner < 2 or chips % inner or chips // inner < 2:
        inner = 2
    return chips // inner, inner


def solution(mesh):
    in_specs = (
        P(None, ("groups", "atoms")),
        P(),
        P(None, ("groups", "atoms"), None),
        P("groups", None, None),
        P(),
        P(("groups", "atoms"), None),
        P(("groups", "atoms")),
    )
    out_specs = (
        P(("groups", "atoms"), None),
        P(None, ("groups", "atoms")),
        P(None, ("groups", "atoms"), None),
    )
    return jax.shard_map(
        functools.partial(body, chip_grid(mesh)),
        mesh=mesh,
        in_specs=in_specs,
        out_specs=out_specs,
        check_vma=False,
    )
```
